256 devices in a mesh: dev: 256 (over x, y, z, core).
Axes of the slice: x: 4, y: 4, z: 8, core: 2. Of those that a mesh axis runs over, the one named last changes fastest.
Arguments:
- state: float32 [5, 8, 8, 8, 32768], P(None, None, None, None, 'dev'), may hold values from -1 to 5, as said below
- neighbours: int32 [6, 32768], P(None, 'dev'), may hold values from 0 to 32767, as said below
Outputs:
- change: float32 [5, 8, 8, 8, 32768], P(None, None, None, None, 'dev')
The draws below stay inside these ranges and needn't reach their ends.
Inputs may be any that keep to these rules, and one draw needn't show every extreme that they name: `state`: component 0 is the density, 1 to 3 the momentum, 4 the total energy of an ideal gas with ratio of heats 1.4; at every node density and pressure lie between 0.6 and 1.8 and each velocity component between -0.4 and 0.4. `neighbours`: device i holds elements i * 128 to (i + 1) * 128 - 1. Across face 2a+1 of element e lies element n exactly when across face 2a of n lies e. Neighbours across faces 0 and 1 lie on the element's own device; across faces 2 and 3 on its own device or on the device whose index differs from it in the lowest bit; across face 5 on the device with index + 2 and across face 4 on the device with index - 2, cyclically. Of one device's faces 2 exactly 8 have their neighbour on another device, and likewise of its faces 3.
All inputs are finite; a program needn't handle non-finite values.
Results may differ from the reference program's by a relative error of at most 0.0001.
Values sent between devices are 32-bit elements; how exact they have to be, the bound alone decides.
A program may use at most 128 MiB of HBM per device.

```python
import jax
import jax.numpy as jnp
import numpy as np
from jax import lax

NODES = 8
LX = 8
HALF_Y = 16
E_DEV = 128
LAYERS = 128
ELEMS = 32768


def draw_state(key, part):
    key = jax.random.fold_in(key, 5)
    keys = jax.random.split(key, 3)
    shape = (NODES, NODES, NODES, ELEMS)
    density = jax.random.uniform(keys[0], shape, minval=0.6, maxval=1.8)
    velocity = jax.random.uniform(keys[1], (3,) + shape, minval=-0.4, maxval=0.4)
    pressure = jax.random.uniform(keys[2], shape, minval=0.6, maxval=1.8)
    momentum = density[None] * velocity
    energy = pressure / 0.4 + 0.5 * density * jnp.sum(velocity * velocity, axis=0)
    return jnp.concatenate([density[None], momentum, energy[None]], axis=0).astype(jnp.float32)


def draw_neighbours(key, part):
    key = jax.random.fold_in(key, 11)
    blocks = ELEMS // E_DEV
    keys = jax.random.split(key, blocks)
    orders = jax.vmap(lambda single: jax.random.permutation(single, E_DEV))(keys).astype(jnp.int32)
    column_x = jnp.arange(LX, dtype=jnp.int32)[:, None, None]
    column_y = jnp.arange(2 * HALF_Y, dtype=jnp.int32)[None, :, None]
    column_z = jnp.arange(LAYERS, dtype=jnp.int32)[None, None, :]
    block = 2 * column_z + column_y // HALF_Y
    position = column_x * HALF_Y + column_y % HALF_Y
    block_full = jnp.broadcast_to(block, (LX, 2 * HALF_Y, LAYERS))
    position_full = jnp.broadcast_to(position, (LX, 2 * HALF_Y, LAYERS))
    ident = block_full * E_DEV + orders[block_full, position_full]
    rolled = []
    for normal in range(3):
        rolled.append(jnp.roll(ident, 1, normal).reshape(-1))
        rolled.append(jnp.roll(ident, -1, normal).reshape(-1))
    result = jnp.zeros((6, ELEMS), jnp.int32)
    return result.at[:, ident.reshape(-1)].set(jnp.stack(rolled)).astype(jnp.int32)


def setup_inputs(seed: int = 0) -> dict:
    key_list = jax.random.split(jax.random.key(seed), 3)
    state = draw_state(jax.random.fold_in(key_list[2], 71), 0)
    neighbours = draw_neighbours(jax.random.fold_in(key_list[2], 71), 0)
    return dict(state=state, neighbours=neighbours)


GAMMA = 1.4
STEP = 0.003
FORMS = ('ai,nijke->najke', 'bj,nijke->nibke', 'ck,nijke->nijce')
LOBATTO_EIGHT = (-1.0, -0.8717401485096066, -0.5917001814331423, -0.2092992179024789, 0.2092992179024789, 0.5917001814331423, 0.8717401485096066, 1.0)

def lobatto_deriv(points_count):
    points = np.array(LOBATTO_EIGHT)
    identity = np.eye(points_count)
    spacing = points[:, None] - points[None, :] + identity
    weights = 1.0 / np.prod(spacing, axis=1)
    matrix = weights[None, :] / weights[:, None] / spacing
    matrix = matrix * (1.0 - identity)
    matrix = matrix - identity * np.sum(matrix, axis=1)[:, None]
    return jnp.asarray(matrix, dtype=jnp.float32)

def primitive(state):
    density = state[0]
    momentum = state[1:4]
    velocity = momentum / density
    pressure = (GAMMA - 1.0) * (state[4] - 0.5 * lax.optimization_barrier(jnp.sum(momentum * velocity, axis=0)))
    return (density, momentum, velocity, pressure)

def flux_rows(state, momentum, velocity, pressure, normal):
    speed_n = velocity[normal]
    rows = [momentum[normal]]
    for column in range(3):
        term = momentum[column] * speed_n
        if column == normal:
            term = term + pressure
        rows.append(term)
    rows.append((state[4] + pressure) * speed_n)
    return jnp.stack(rows)

def normal_flux(state, normal):
    density, momentum, velocity, pressure = primitive(state)
    fluxes = flux_rows(state, momentum, velocity, pressure, normal)
    wave = jnp.abs(velocity[normal]) + jnp.sqrt(GAMMA * pressure / density)
    return (fluxes, wave)

def rusanov(left, right, normal):
    flux_left, wave_left = normal_flux(left, normal)
    flux_right, wave_right = normal_flux(right, normal)
    wave = jnp.maximum(wave_left, wave_right)
    return 0.5 * (flux_left + flux_right) - 0.5 * wave * (right - left)

def face(field, normal, sided):
    return lax.index_in_dim(field, sided * (field.shape[1] - 1), 1 + normal, keepdims=False)

def volume_part(state, deriv):
    density, momentum, velocity, pressure = primitive(state)
    rate = jnp.zeros_like(state)
    own_lower = []
    own_upper = []
    for normal in range(3):
        fluxes = flux_rows(state, momentum, velocity, pressure, normal)
        rate = rate - jnp.einsum(FORMS[normal], deriv, fluxes, precision=lax.Precision.HIGHEST)
        own_lower.append(face(fluxes, normal, 0))
        own_upper.append(face(fluxes, normal, 1))
    return (rate, own_lower, own_upper)

def add_surface(rate, own_lower, own_upper, lower_star, upper_star):
    last = rate.shape[1] - 1
    lift = last * (last + 1) / 2.0
    for normal in range(3):
        upper_idx = (slice(None),) * (1 + normal) + (last,)
        lower_idx = (slice(None),) * (1 + normal) + (0,)
        rate = rate.at[upper_idx].add(lift * (own_upper[normal] - upper_star[normal]))
        rate = rate.at[lower_idx].add(lift * (lower_star[normal] - own_lower[normal]))
    return rate

def tendency(state, neighbours, deriv):
    rate, own_lower, own_upper = volume_part(state, deriv)
    upper_star = []
    lower_star = []
    for normal in range(3):
        lower = face(state, normal, 0)
        upper = face(state, normal, 1)
        across = jnp.take(lower, neighbours[2 * normal + 1], axis=-1)
        star = rusanov(upper, across, normal)
        upper_star.append(star)
        lower_star.append(jnp.take(star, neighbours[2 * normal], axis=-1))
    return add_surface(rate, own_lower, own_upper, lower_star, upper_star)

def reference(state, neighbours):
    deriv = lobatto_deriv(state.shape[1])
    rate_start = tendency(state, neighbours, deriv)
    first = state + STEP * rate_start
    rate_first = tendency(first, neighbours, deriv)
    return 0.5 * STEP * (rate_start + rate_first)
```

```python
import functools

import jax
import jax.numpy as jnp
import numpy as np
from jax import lax
from jax.experimental import pallas as pl
from jax.experimental.pallas import tpu as pltpu
from jax.sharding import PartitionSpec as P

MESH = pl.DeviceIdType.MESH
GAMMA = 1.4
STEP = 0.003
NODES = 8
ELEMS = 128
LAST = NODES - 1
LIFT = LAST * (LAST + 1) / 2.0
LOBATTO_EIGHT = (
    -1.0,
    -0.8717401485096066,
    -0.5917001814331423,
    -0.2092992179024789,
    0.2092992179024789,
    0.5917001814331423,
    0.8717401485096066,
    1.0,
)


def folded_matrix():
    points = np.array(LOBATTO_EIGHT)
    identity = np.eye(NODES)
    spacing = points[:, None] - points[None, :] + identity
    weights = 1.0 / np.prod(spacing, axis=1)
    matrix = weights[None, :] / weights[:, None] / spacing
    matrix = matrix * (1.0 - identity)
    matrix = matrix - identity * np.sum(matrix, axis=1)[:, None]
    matrix = -matrix
    matrix[LAST, LAST] += LIFT
    matrix[0, 0] -= LIFT
    return matrix


MATRIX = folded_matrix()
EVEN = 0.5 * (MATRIX[:4, :4] + MATRIX[:4, :3:-1])
ODD = 0.5 * (MATRIX[:4, :4] - MATRIX[:4, :3:-1])


def derivative(values):
    even = [values[j] + values[LAST - j] for j in range(4)]
    odd = [values[j] - values[LAST - j] for j in range(4)]
    result = [None] * NODES
    for i in range(4):
        a = even[0] * float(EVEN[i, 0])
        b = odd[0] * float(ODD[i, 0])
        for j in range(1, 4):
            a = a + even[j] * float(EVEN[i, j])
            b = b + odd[j] * float(ODD[i, j])
        result[i] = b + a
        result[LAST - i] = b - a
    return result


def primitive(q):
    inverse = 1.0 / q[0]
    v = [q[1] * inverse, q[2] * inverse, q[3] * inverse]
    p = (GAMMA - 1.0) * (q[4] - 0.5 * (q[1] * v[0] + q[2] * v[1] + q[3] * v[2]))
    return inverse, v, p


def side(q, normal):
    inverse, v, p = primitive(q)
    speed = v[normal]
    flux = [q[1 + normal]]
    for column in range(3):
        term = q[1 + column] * speed
        flux.append(term + p if column == normal else term)
    flux.append((q[4] + p) * speed)
    wave = jnp.abs(speed) + jnp.sqrt(GAMMA * p * inverse)
    return flux, wave


def rusanov(left, right, normal):
    flux_left, wave_left = side(left, normal)
    flux_right, wave_right = side(right, normal)
    wave = jnp.maximum(wave_left, wave_right)
    return [
        0.5 * ((flux_left[c] + flux_right[c]) - wave * (right[c] - left[c])) for c in range(5)
    ]


def pick(table, columns):
    return jnp.take_along_axis(table, columns, axis=1, mode="promise_in_bounds")


def kernel(
    devices,
    state_hbm,
    neighbours_ref,
    out_hbm,
    u,
    r,
    prim,
    index,
    send_z,
    recv_z,
    recv_y,
    star_z,
    in_sem,
    out_sem,
    send_sem,
    recv_sem,
):
    me = lax.axis_index("dev")
    above = lax.rem(me + 2, devices)
    below = lax.rem(me + devices - 2, devices)
    partner = me + 1 - 2 * lax.rem(me, 2)

    load = pltpu.make_async_copy(state_hbm, u, in_sem)
    load.start()

    barrier = pltpu.get_barrier_semaphore()
    for other in (above, below, partner):
        pl.semaphore_signal(barrier, inc=1, device_id=(other,), device_id_type=MESH)

    ids = neighbours_ref[...]
    local = jnp.bitwise_and(ids, ELEMS - 1)
    remote = (jnp.right_shift(ids, 7) != me).astype(jnp.int32)
    for f in range(6):
        index[f] = jnp.broadcast_to(local[f : f + 1], (8, ELEMS))
    index[6] = jnp.broadcast_to(remote[2:3], (8, ELEMS))
    index[7] = jnp.broadcast_to(remote[3:4], (8, ELEMS))

    pl.semaphore_wait(barrier, 3)
    load.wait()

    def send(slot, source, target, device):
        copy = pltpu.make_async_remote_copy(
            src_ref=source,
            dst_ref=target,
            send_sem=send_sem.at[slot],
            recv_sem=recv_sem.at[slot],
            device_id=(device,),
            device_id_type=MESH,
        )
        copy.start()
        return copy

    def rows_j(j):
        return pl.ds(j * 8, 8)

    def rows_k(k):
        return pl.ds(k, 8, stride=8)

    def send_y(section):
        lower = send(4 + 2 * section, u.at[:, :, pl.ds(0, 8)], recv_y.at[2 * section], partner)
        upper = send(5 + 2 * section, u.at[:, :, pl.ds(56, 8)], recv_y.at[2 * section + 1], partner)
        return lower, upper

    def pack(i, carry):
        for c in range(5):
            send_z[0, c, i] = u[c, i, rows_k(0)]
            send_z[1, c, i] = u[c, i, rows_k(LAST)]
        return carry

    lax.fori_loop(0, 8, pack, 0)
    z_copies = [
        send(0, send_z.at[0], recv_z.at[0], below),
        send(1, send_z.at[1], recv_z.at[1], above),
    ]
    y_copies = [send_y(0)]

    def volume(section):
        def slab(i, carry):
            for j in range(8):
                q = [u[c, i, rows_j(j)] for c in range(5)]
                if section:
                    q = [q[c] + STEP * r[c, i, rows_j(j)] for c in range(5)]
                    for c in range(5):
                        u[c, i, rows_j(j)] = q[c]
                _, v, p = primitive(q)
                for d in range(3):
                    prim[d, i, rows_j(j)] = v[d]
                prim[3, i, rows_j(j)] = p
                prim[4, i, rows_j(j)] = q[4] + p
            return carry

        lax.fori_loop(0, 8, slab, 0)
        if section:
            y_copies.append(send_y(1))

        def fluxes(normal, at):
            speed = None
            for c in range(5):
                if c == 0:
                    yield c, [u[1 + normal, *at(n)] for n in range(8)]
                    continue
                if speed is None:
                    speed = [prim[normal, *at(n)] for n in range(8)]
                if c == 4:
                    yield c, [prim[4, *at(n)] * speed[n] for n in range(8)]
                    continue
                flux = [u[c, *at(n)] * speed[n] for n in range(8)]
                if c == 1 + normal:
                    flux = [flux[n] + prim[3, *at(n)] for n in range(8)]
                yield c, flux

        def along_j(i, carry):
            at = lambda n: (i, rows_j(n))
            for c, flux in fluxes(1, at):
                rate = derivative(flux)
                for n in range(8):
                    if section:
                        r[c, *at(n)] += rate[n]
                    else:
                        r[c, *at(n)] = rate[n]
            at_k = lambda n: (i, rows_k(n))
            for c, flux in fluxes(2, at_k):
                rate = derivative(flux)
                for n in range(8):
                    r[c, *at_k(n)] = r[c, *at_k(n)] + rate[n]
            return carry

        lax.fori_loop(0, 8, along_j, 0)

        def along_i(j, carry):
            rows = pl.ds(pl.multiple_of(j * 8, 8), 8)
            at = lambda n: (n, rows)
            for c, flux in fluxes(0, at):
                rate = derivative(flux)
                for n in range(8):
                    r[c, *at(n)] += rate[n]
            return carry

        lax.fori_loop(0, 8, along_i, 0)

    def surface_x():
        def face(j, carry):
            rows = pl.ds(pl.multiple_of(j * 8, 8), 8)
            left = [u[c, LAST, rows] for c in range(5)]
            right = [pick(u[c, 0, rows], index[1]) for c in range(5)]
            star = rusanov(left, right, 0)
            for c in range(5):
                lifted = LIFT * star[c]
                r[c, LAST, rows] -= lifted
                r[c, 0, rows] += pick(lifted, index[0])
            return carry

        lax.fori_loop(0, 8, face, 0)

    def surface_y(section):
        for copy in y_copies[section]:
            copy.wait_recv()
        got_lower = recv_y.at[2 * section]
        got_upper = recv_y.at[2 * section + 1]

        def face(i, carry):
            lower = [u[c, i, rows_j(0)] for c in range(5)]
            upper = [u[c, i, rows_j(LAST)] for c in range(5)]
            remote_low = index[6] != 0
            remote_up = index[7] != 0
            right = [
                jnp.where(remote_up, pick(got_lower[c, i], index[3]), pick(lower[c], index[3]))
                for c in range(5)
            ]
            star = rusanov(upper, right, 1)
            for c in range(5):
                r[c, i, rows_j(LAST)] -= LIFT * star[c]
            left = [
                jnp.where(remote_low, pick(got_upper[c, i], index[2]), pick(upper[c], index[2]))
                for c in range(5)
            ]
            star = rusanov(left, lower, 1)
            for c in range(5):
                r[c, i, rows_j(0)] += LIFT * star[c]
            return carry

        lax.fori_loop(0, 8, face, 0)

    def surface_z(section):
        def face(i, carry):
            left = [u[c, i, rows_k(LAST)] for c in range(5)]
            right = [pick(recv_z[2 * section, c, i], index[5]) for c in range(5)]
            if section:
                right = [right[c] + STEP * star_z[0, c, i] for c in range(5)]
            star = rusanov(left, right, 2)
            for c in range(5):
                lifted = LIFT * star[c]
                r[c, i, rows_k(LAST)] = r[c, i, rows_k(LAST)] - lifted
                if not section:
                    star_z[0, c, i] = lifted
            left = [pick(recv_z[2 * section + 1, c, i], index[4]) for c in range(5)]
            if section:
                left = [left[c] - STEP * star_z[1, c, i] for c in range(5)]
            right = [u[c, i, rows_k(0)] for c in range(5)]
            star = rusanov(left, right, 2)
            for c in range(5):
                lifted = LIFT * star[c]
                r[c, i, rows_k(0)] = r[c, i, rows_k(0)] + lifted
                if not section:
                    star_z[1, c, i] = lifted
            if section:
                for c in range(5):
                    r[c, i] = (0.5 * STEP) * r[c, i]
            return carry

        lax.fori_loop(0, 8, face, 0)

    volume(0)
    surface_x()
    surface_y(0)

    def pack_again(i, carry):
        for c in range(5):
            for s, k in ((0, 0), (1, LAST)):
                send_z[2 + s, c, i] = u[c, i, rows_k(k)] + STEP * r[c, i, rows_k(k)]
        return carry

    lax.fori_loop(0, 8, pack_again, 0)
    z_copies += [
        send(2, send_z.at[2], recv_z.at[2], below),
        send(3, send_z.at[3], recv_z.at[3], above),
    ]
    for copy in z_copies[:2]:
        copy.wait_recv()
    surface_z(0)
    for copy in y_copies[0]:
        copy.wait_send()

    volume(1)
    surface_x()
    surface_y(1)
    for copy in z_copies[2:]:
        copy.wait_recv()
    surface_z(1)

    store = pltpu.make_async_copy(r, out_hbm, out_sem)
    store.start()
    for copy in z_copies:
        copy.wait_send()
    for copy in y_copies[1]:
        copy.wait_send()
    store.wait()


def body(devices, state, neighbours):
    flat = state.reshape(5, 8, 64, ELEMS)
    change = pl.pallas_call(
        functools.partial(kernel, devices),
        out_shape=jax.ShapeDtypeStruct(flat.shape, jnp.float32),
        in_specs=[pl.BlockSpec(memory_space=pl.ANY), pl.BlockSpec(memory_space=pltpu.VMEM)],
        out_specs=pl.BlockSpec(memory_space=pl.ANY),
        scratch_shapes=[
            pltpu.VMEM((5, 8, 64, ELEMS), jnp.float32),
            pltpu.VMEM((5, 8, 64, ELEMS), jnp.float32),
            pltpu.VMEM((5, 8, 64, ELEMS), jnp.float32),
            pltpu.VMEM((8, 8, ELEMS), jnp.int32),
            pltpu.VMEM((4, 5, 8, 8, ELEMS), jnp.float32),
            pltpu.VMEM((4, 5, 8, 8, ELEMS), jnp.float32),
            pltpu.VMEM((4, 5, 8, 8, ELEMS), jnp.float32),
            pltpu.VMEM((2, 5, 8, 8, ELEMS), jnp.float32),
            pltpu.SemaphoreType.DMA,
            pltpu.SemaphoreType.DMA,
            pltpu.SemaphoreType.DMA((8,)),
            pltpu.SemaphoreType.DMA((8,)),
        ],
        compiler_params=pltpu.CompilerParams(
            collective_id=0, has_side_effects=True, vmem_limit_bytes=40 * 1024 * 1024
        ),
        cost_estimate=pl.CostEstimate(
            flops=25_000_000, bytes_accessed=2_700_000, transcendentals=0
        ),
    )(flat, neighbours)
    return change.reshape(state.shape)


def solution(mesh):
    devices = mesh.shape["dev"]
    in_specs = (P(None, None, None, None, "dev"), P(None, "dev"))
    out_specs = P(None, None, None, None, "dev")
    return jax.shard_map(
        functools.partial(body, devices),
        mesh=mesh,
        in_specs=in_specs,
        out_specs=out_specs,
        check_vma=False,
    )
```

```python
import functools

import jax
import jax.numpy as jnp
import numpy as np
from jax import lax
from jax.experimental import pallas as pl
from jax.experimental.pallas import tpu as pltpu
from jax.sharding import PartitionSpec as P

MESH = pl.DeviceIdType.MESH
GAMMA = 1.4
STEP = 0.003
NODES = 8
ELEMS = 128
LAST = NODES - 1
LIFT = LAST * (LAST + 1) / 2.0
LOBATTO_EIGHT = (
    -1.0,
    -0.8717401485096066,
    -0.5917001814331423,
    -0.2092992179024789,
    0.2092992179024789,
    0.5917001814331423,
    0.8717401485096066,
    1.0,
)


def folded_matrix():
    points = np.array(LOBATTO_EIGHT)
    identity = np.eye(NODES)
    spacing = points[:, None] - points[None, :] + identity
    weights = 1.0 / np.prod(spacing, axis=1)
    matrix = weights[None, :] / weights[:, None] / spacing
    matrix = matrix * (1.0 - identity)
    matrix = matrix - identity * np.sum(matrix, axis=1)[:, None]
    matrix = -matrix
    matrix[LAST, LAST] += LIFT
    matrix[0, 0] -= LIFT
    return matrix


MATRIX = folded_matrix()
EVEN = 0.5 * (MATRIX[:4, :4] + MATRIX[:4, :3:-1])
ODD = 0.5 * (MATRIX[:4, :4] - MATRIX[:4, :3:-1])


def derivative(values):
    even = [values[j] + values[LAST - j] for j in range(4)]
    odd = [values[j] - values[LAST - j] for j in range(4)]
    result = [None] * NODES
    for i in range(4):
        a = even[0] * float(EVEN[i, 0])
        b = odd[0] * float(ODD[i, 0])
        for j in range(1, 4):
            a = a + even[j] * float(EVEN[i, j])
            b = b + odd[j] * float(ODD[i, j])
        result[i] = b + a
        result[LAST - i] = b - a
    return result


def primitive(q):
    inverse = 1.0 / q[0]
    v = [q[1] * inverse, q[2] * inverse, q[3] * inverse]
    p = (GAMMA - 1.0) * (q[4] - 0.5 * (q[1] * v[0] + q[2] * v[1] + q[3] * v[2]))
    return inverse, v, p


def side(q, normal):
    inverse, v, p = primitive(q)
    speed = v[normal]
    flux = [q[1 + normal]]
    for column in range(3):
        term = q[1 + column] * speed
        flux.append(term + p if column == normal else term)
    flux.append((q[4] + p) * speed)
    wave = jnp.abs(speed) + jnp.sqrt(GAMMA * p * inverse)
    return flux, wave


def rusanov(left, right, normal):
    flux_left, wave_left = side(left, normal)
    flux_right, wave_right = side(right, normal)
    wave = jnp.maximum(wave_left, wave_right)
    return [
        0.5 * ((flux_left[c] + flux_right[c]) - wave * (right[c] - left[c])) for c in range(5)
    ]


def pick(table, columns):
    return jnp.take_along_axis(table, columns, axis=1, mode="promise_in_bounds")


def kernel(
    devices,
    state_hbm,
    neighbours_hbm,
    r,
    u,
    prim,
    ids_ref,
    index,
    send_z,
    recv_z,
    recv_y,
    star_z,
    in_sem,
    send_sem,
    recv_sem,
):
    me = lax.axis_index("dev")
    above = lax.rem(me + 2, devices)
    below = lax.rem(me + devices - 2, devices)
    partner = me + 1 - 2 * lax.rem(me, 2)

    loads = [
        pltpu.make_async_copy(state_hbm.at[:, i], u.at[:, i], in_sem.at[i]) for i in range(8)
    ]
    for load in loads:
        load.start()
    load_ids = pltpu.make_async_copy(neighbours_hbm, ids_ref, in_sem.at[8])
    load_ids.start()

    barrier = pltpu.get_barrier_semaphore()
    for other in (above, below, partner):
        pl.semaphore_signal(barrier, inc=1, device_id=(other,), device_id_type=MESH)

    load_ids.wait()
    ids = ids_ref[...]
    local = jnp.bitwise_and(ids, ELEMS - 1)
    remote = (jnp.right_shift(ids, 7) != me).astype(jnp.int32)
    for f in range(6):
        index[f] = jnp.broadcast_to(local[f : f + 1], (8, ELEMS))
    index[6] = jnp.broadcast_to(remote[2:3], (8, ELEMS))
    index[7] = jnp.broadcast_to(remote[3:4], (8, ELEMS))


    def send(slot, source, target, device):
        copy = pltpu.make_async_remote_copy(
            src_ref=source,
            dst_ref=target,
            send_sem=send_sem.at[slot],
            recv_sem=recv_sem.at[slot],
            device_id=(device,),
            device_id_type=MESH,
        )
        copy.start()
        return copy

    def rows_j(j):
        return pl.ds(j * 8, 8)

    def rows_k(k):
        return pl.ds(k, 8, stride=8)

    def send_y(section):
        lower = send(4 + 2 * section, u.at[:, :, pl.ds(0, 8)], recv_y.at[2 * section], partner)
        upper = send(5 + 2 * section, u.at[:, :, pl.ds(56, 8)], recv_y.at[2 * section + 1], partner)
        return lower, upper

    for i in range(8):
        loads[i].wait()
        for c in range(5):
            send_z[0, c, i] = u[c, i, rows_k(0)]
            send_z[1, c, i] = u[c, i, rows_k(LAST)]
    pl.semaphore_wait(barrier, 3)
    z_copies = [
        send(0, send_z.at[0], recv_z.at[0], below),
        send(1, send_z.at[1], recv_z.at[1], above),
    ]
    y_copies = [send_y(0)]

    def volume(section):
        def slab(i, carry):
            for j in range(8):
                q = [u[c, i, rows_j(j)] for c in range(5)]
                if section:
                    q = [q[c] + STEP * r[c, i, rows_j(j)] for c in range(5)]
                    for c in range(5):
                        u[c, i, rows_j(j)] = q[c]
                _, v, p = primitive(q)
                for d in range(3):
                    prim[d, i, rows_j(j)] = v[d]
                prim[3, i, rows_j(j)] = p
                prim[4, i, rows_j(j)] = q[4] + p
            return carry

        lax.fori_loop(0, 8, slab, 0)
        if section:
            y_copies.append(send_y(1))

        def fluxes(normal, at):
            speed = None
            for c in range(5):
                if c == 0:
                    yield c, [u[1 + normal, *at(n)] for n in range(8)]
                    continue
                if speed is None:
                    speed = [prim[normal, *at(n)] for n in range(8)]
                if c == 4:
                    yield c, [prim[4, *at(n)] * speed[n] for n in range(8)]
                    continue
                flux = [u[c, *at(n)] * speed[n] for n in range(8)]
                if c == 1 + normal:
                    flux = [flux[n] + prim[3, *at(n)] for n in range(8)]
                yield c, flux

        def along_j(i, carry):
            at = lambda n: (i, rows_j(n))
            for c, flux in fluxes(1, at):
                rate = derivative(flux)
                for n in range(8):
                    if section:
                        r[c, *at(n)] += rate[n]
                    else:
                        r[c, *at(n)] = rate[n]
            at_k = lambda n: (i, rows_k(n))
            for c, flux in fluxes(2, at_k):
                rate = derivative(flux)
                for n in range(8):
                    r[c, *at_k(n)] = r[c, *at_k(n)] + rate[n]
            return carry

        lax.fori_loop(0, 8, along_j, 0)

        def along_i(j, carry):
            rows = pl.ds(pl.multiple_of(j * 8, 8), 8)
            at = lambda n: (n, rows)
            for c, flux in fluxes(0, at):
                rate = derivative(flux)
                for n in range(8):
                    r[c, *at(n)] += rate[n]
            return carry

        lax.fori_loop(0, 8, along_i, 0)

    def surface_x():
        def face(j, carry):
            rows = pl.ds(pl.multiple_of(j * 8, 8), 8)
            left = [u[c, LAST, rows] for c in range(5)]
            right = [pick(u[c, 0, rows], index[1]) for c in range(5)]
            star = rusanov(left, right, 0)
            for c in range(5):
                lifted = LIFT * star[c]
                r[c, LAST, rows] -= lifted
                r[c, 0, rows] += pick(lifted, index[0])
            return carry

        lax.fori_loop(0, 8, face, 0, unroll=8)

    def surface_y(section):
        for copy in y_copies[section]:
            copy.wait_recv()
        got_lower = recv_y.at[2 * section]
        got_upper = recv_y.at[2 * section + 1]

        def face(i, carry):
            lower = [u[c, i, rows_j(0)] for c in range(5)]
            upper = [u[c, i, rows_j(LAST)] for c in range(5)]
            remote_low = index[6] != 0
            remote_up = index[7] != 0
            right = [
                jnp.where(remote_up, pick(got_lower[c, i], index[3]), pick(lower[c], index[3]))
                for c in range(5)
            ]
            star = rusanov(upper, right, 1)
            for c in range(5):
                r[c, i, rows_j(LAST)] -= LIFT * star[c]
            left = [
                jnp.where(remote_low, pick(got_upper[c, i], index[2]), pick(upper[c], index[2]))
                for c in range(5)
            ]
            star = rusanov(left, lower, 1)
            for c in range(5):
                r[c, i, rows_j(0)] += LIFT * star[c]
            return carry

        lax.fori_loop(0, 8, face, 0, unroll=8)

    def surface_z(section):
        def face(i, carry):
            left = [u[c, i, rows_k(LAST)] for c in range(5)]
            right = [pick(recv_z[2 * section, c, i], index[5]) for c in range(5)]
            if section:
                right = [right[c] + STEP * star_z[0, c, i] for c in range(5)]
            star = rusanov(left, right, 2)
            for c in range(5):
                lifted = LIFT * star[c]
                r[c, i, rows_k(LAST)] = r[c, i, rows_k(LAST)] - lifted
                if not section:
                    star_z[0, c, i] = lifted
            left = [pick(recv_z[2 * section + 1, c, i], index[4]) for c in range(5)]
            if section:
                left = [left[c] - STEP * star_z[1, c, i] for c in range(5)]
            right = [u[c, i, rows_k(0)] for c in range(5)]
            star = rusanov(left, right, 2)
            for c in range(5):
                lifted = LIFT * star[c]
                r[c, i, rows_k(0)] = r[c, i, rows_k(0)] + lifted
                if not section:
                    star_z[1, c, i] = lifted
            if section:
                for c in range(5):
                    r[c, i] = (0.5 * STEP) * r[c, i]
            return carry

        lax.fori_loop(0, 8, face, 0, unroll=8)

    volume(0)
    surface_x()
    surface_y(0)

    def pack_again(i, carry):
        for c in range(5):
            for s, k in ((0, 0), (1, LAST)):
                send_z[2 + s, c, i] = u[c, i, rows_k(k)] + STEP * r[c, i, rows_k(k)]
        return carry

    lax.fori_loop(0, 8, pack_again, 0, unroll=8)
    z_copies += [
        send(2, send_z.at[2], recv_z.at[2], below),
        send(3, send_z.at[3], recv_z.at[3], above),
    ]
    for copy in z_copies[:2]:
        copy.wait_recv()
    surface_z(0)
    for copy in y_copies[0]:
        copy.wait_send()

    volume(1)
    surface_x()
    surface_y(1)
    for copy in z_copies[2:]:
        copy.wait_recv()
    surface_z(1)

    for copy in z_copies:
        copy.wait_send()
    for copy in y_copies[1]:
        copy.wait_send()


def body(devices, state, neighbours):
    flat = state.reshape(5, 8, 64, ELEMS)
    change = pl.pallas_call(
        functools.partial(kernel, devices),
        out_shape=pltpu.VMEM(flat.shape, jnp.float32),
        in_specs=[pl.BlockSpec(memory_space=pltpu.HBM), pl.BlockSpec(memory_space=pltpu.HBM)],
        out_specs=pl.BlockSpec(memory_space=pltpu.VMEM),
        scratch_shapes=[
            pltpu.VMEM((5, 8, 64, ELEMS), jnp.float32),
            pltpu.VMEM((5, 8, 64, ELEMS), jnp.float32),
            pltpu.VMEM((6, ELEMS), jnp.int32),
            pltpu.VMEM((8, 8, ELEMS), jnp.int32),
            pltpu.VMEM((4, 5, 8, 8, ELEMS), jnp.float32),
            pltpu.VMEM((4, 5, 8, 8, ELEMS), jnp.float32),
            pltpu.VMEM((4, 5, 8, 8, ELEMS), jnp.float32),
            pltpu.VMEM((2, 5, 8, 8, ELEMS), jnp.float32),
            pltpu.SemaphoreType.DMA((9,)),
            pltpu.SemaphoreType.DMA((8,)),
            pltpu.SemaphoreType.DMA((8,)),
        ],
        compiler_params=pltpu.CompilerParams(
            collective_id=0, has_side_effects=True, vmem_limit_bytes=40 * 1024 * 1024
        ),
        cost_estimate=pl.CostEstimate(
            flops=25_000_000, bytes_accessed=2_700_000, transcendentals=0
        ),
    )(
        pltpu.with_memory_space_constraint(flat, pltpu.HBM),
        pltpu.with_memory_space_constraint(neighbours, pltpu.HBM),
    )
    return change.reshape(state.shape)


def solution(mesh):
    devices = mesh.shape["dev"]
    in_specs = (P(None, None, None, None, "dev"), P(None, "dev"))
    out_specs = P(None, None, None, None, "dev")
    return jax.shard_map(
        functools.partial(body, devices),
        mesh=mesh,
        in_specs=in_specs,
        out_specs=out_specs,
        check_vma=False,
    )
```

```python
import functools

import jax
import jax.numpy as jnp
import numpy as np
from jax import lax
from jax.experimental import pallas as pl
from jax.experimental.pallas import tpu as pltpu
from jax.sharding import PartitionSpec as P

MESH = pl.DeviceIdType.MESH
GAMMA = 1.4
STEP = 0.003
NODES = 8
ELEMS = 128
LAST = NODES - 1
LIFT = LAST * (LAST + 1) / 2.0
ENDS = (0, LAST)
MIDDLE = tuple(range(1, LAST))
LOBATTO_EIGHT = (
    -1.0,
    -0.8717401485096066,
    -0.5917001814331423,
    -0.2092992179024789,
    0.2092992179024789,
    0.5917001814331423,
    0.8717401485096066,
    1.0,
)


def folded_matrix():
    points = np.array(LOBATTO_EIGHT)
    identity = np.eye(NODES)
    spacing = points[:, None] - points[None, :] + identity
    weights = 1.0 / np.prod(spacing, axis=1)
    matrix = weights[None, :] / weights[:, None] / spacing
    matrix = matrix * (1.0 - identity)
    matrix = matrix - identity * np.sum(matrix, axis=1)[:, None]
    matrix = -matrix
    matrix[LAST, LAST] += LIFT
    matrix[0, 0] -= LIFT
    return matrix


MATRIX = folded_matrix()
EVEN = 0.5 * (MATRIX[:4, :4] + MATRIX[:4, :3:-1])
ODD = 0.5 * (MATRIX[:4, :4] - MATRIX[:4, :3:-1])


def derivative(values, pairs=(0, 1, 2, 3)):
    even = {j: values[j] + values[LAST - j] for j in pairs}
    odd = {j: values[j] - values[LAST - j] for j in pairs}
    result = [None] * NODES
    for i in range(4):
        a = b = None
        for j in pairs:
            x = even[j] * float(EVEN[i, j])
            y = odd[j] * float(ODD[i, j])
            a = x if a is None else a + x
            b = y if b is None else b + y
        result[i] = b + a
        result[LAST - i] = b - a
    return result


def primitive(q):
    inverse = 1.0 / q[0]
    v = [q[1] * inverse, q[2] * inverse, q[3] * inverse]
    p = (GAMMA - 1.0) * (q[4] - 0.5 * (q[1] * v[0] + q[2] * v[1] + q[3] * v[2]))
    return inverse, v, p


def side(q, normal):
    inverse, v, p = primitive(q)
    speed = v[normal]
    flux = [q[1 + normal]]
    for column in range(3):
        term = q[1 + column] * speed
        flux.append(term + p if column == normal else term)
    flux.append((q[4] + p) * speed)
    wave = jnp.abs(speed) + jnp.sqrt(GAMMA * p * inverse)
    return flux, wave


def rusanov(left, right, normal):
    flux_left, wave_left = side(left, normal)
    flux_right, wave_right = side(right, normal)
    wave = jnp.maximum(wave_left, wave_right)
    return [
        0.5 * ((flux_left[c] + flux_right[c]) - wave * (right[c] - left[c])) for c in range(5)
    ]


def pick(table, columns):
    return jnp.take_along_axis(table, columns, axis=1, mode="promise_in_bounds")


def kernel(
    devices,
    state_hbm,
    neighbours_hbm,
    out,
    planes,
    r,
    prim,
    ids_ref,
    index,
    ends,
    recv_z,
    star_z,
    own_y_ends,
    own_y_middle,
    recv_y_ends,
    recv_y_middle,
    in_sem,
    send_sem,
    recv_sem,
):
    u = planes.reshape(5, 8, 64, ELEMS)
    me = lax.axis_index("dev")
    above = lax.rem(me + 2, devices)
    below = lax.rem(me + devices - 2, devices)
    partner = me + 1 - 2 * lax.rem(me, 2)

    loads = {
        k: pltpu.make_async_copy(state_hbm.at[:, :, :, k, :], planes.at[:, k], in_sem.at[k])
        for k in ENDS + MIDDLE
    }
    for load in loads.values():
        load.start()
    load_ids = pltpu.make_async_copy(neighbours_hbm, ids_ref, in_sem.at[8])
    load_ids.start()

    barrier = pltpu.get_barrier_semaphore()
    for other in (above, below, partner):
        pl.semaphore_signal(barrier, inc=1, device_id=(other,), device_id_type=MESH)

    def send(slot, source, target, device):
        copy = pltpu.make_async_remote_copy(
            src_ref=source,
            dst_ref=target,
            send_sem=send_sem.at[slot],
            recv_sem=recv_sem.at[slot],
            device_id=(device,),
            device_id_type=MESH,
        )
        copy.start()
        return copy

    def rows_i(i):
        if isinstance(i, int):
            return pl.ds(i * 8, 8)
        return pl.ds(pl.multiple_of(i * 8, 8), 8)

    def rows_j(j):
        return pl.ds(j, 8, stride=8)

    def rows_k(k):
        return pl.ds(k, 8, stride=8)

    def send_y(section, which):
        own, got, which_planes, slot = (
            (own_y_ends, recv_y_ends, ENDS, 4 + section)
            if which == ENDS
            else (own_y_middle, recv_y_middle, MIDDLE, 6 + section)
        )
        for n, k in enumerate(which_planes):
            for c in range(5):
                for side_y, j in ((0, 0), (1, LAST)):
                    own[section, side_y, c, n] = u[c, k, rows_j(j)]
        return send(slot, own.at[section], got.at[section], partner)

    def primitives(k, update):
        for i in range(8):
            q = [u[c, k, rows_i(i)] for c in range(5)]
            if update:
                q = [q[c] + STEP * r[c, k, rows_i(i)] for c in range(5)]
                for c in range(5):
                    u[c, k, rows_i(i)] = q[c]
            _, v, p = primitive(q)
            for d in range(3):
                prim[d, k, rows_i(i)] = v[d]
            prim[3, k, rows_i(i)] = p
            prim[4, k, rows_i(i)] = q[4] + p

    def fluxes(normal, at, nodes=tuple(range(8))):
        speed = {n: prim[normal, *at(n)] for n in nodes}
        for c in range(5):
            if c == 0:
                yield c, {n: u[1 + normal, *at(n)] for n in nodes}
                continue
            if c == 4:
                yield c, {n: prim[4, *at(n)] * speed[n] for n in nodes}
                continue
            flux = {n: u[c, *at(n)] * speed[n] for n in nodes}
            if c == 1 + normal:
                flux = {n: flux[n] + prim[3, *at(n)] for n in nodes}
            yield c, flux

    def in_plane(k):
        for normal, rows in ((0, rows_i), (1, rows_j)):
            at = lambda n: (k, rows(n))
            for c, flux in fluxes(normal, at):
                rate = derivative(flux)
                for n in range(8):
                    r[c, *at(n)] = r[c, *at(n)] + rate[n]

    def surface_x(k):
        left = [u[c, k, rows_i(LAST)] for c in range(5)]
        right = [pick(u[c, k, rows_i(0)], index[1]) for c in range(5)]
        star = rusanov(left, right, 0)
        for c in range(5):
            lifted = LIFT * star[c]
            r[c, k, rows_i(LAST)] -= lifted
            r[c, k, rows_i(0)] += pick(lifted, index[0])

    def surface_y(section, which):
        own, got, which_planes = (
            (own_y_ends, recv_y_ends, ENDS)
            if which == ENDS
            else (own_y_middle, recv_y_middle, MIDDLE)
        )
        for n, k in enumerate(which_planes):
            lower = [own[section, 0, c, n] for c in range(5)]
            upper = [own[section, 1, c, n] for c in range(5)]
            remote_low = index[6] != 0
            remote_up = index[7] != 0
            right = [
                jnp.where(
                    remote_up, pick(got[section, 0, c, n], index[3]), pick(lower[c], index[3])
                )
                for c in range(5)
            ]
            star = rusanov(upper, right, 1)
            for c in range(5):
                r[c, k, rows_j(LAST)] = r[c, k, rows_j(LAST)] - LIFT * star[c]
            left = [
                jnp.where(
                    remote_low, pick(got[section, 1, c, n], index[2]), pick(upper[c], index[2])
                )
                for c in range(5)
            ]
            star = rusanov(left, lower, 1)
            for c in range(5):
                r[c, k, rows_j(0)] = r[c, k, rows_j(0)] + LIFT * star[c]

    def loop(first, last, step, unroll=1):
        def wrapped(n, carry):
            step(n)
            return carry

        lax.fori_loop(first, last, wrapped, 0, unroll=unroll)

    for k in ENDS:
        loads[k].wait()
    pl.semaphore_wait(barrier, 3)
    z_copies = [
        send(0, planes.at[:, 0], recv_z.at[0], below),
        send(1, planes.at[:, LAST], recv_z.at[1], above),
    ]
    y_copies = [send_y(0, ENDS)]

    load_ids.wait()
    ids = ids_ref[...]
    local = jnp.bitwise_and(ids, ELEMS - 1)
    remote = (jnp.right_shift(ids, 7) != me).astype(jnp.int32)
    for f in range(6):
        index[f] = jnp.broadcast_to(local[f : f + 1], (8, ELEMS))
    index[6] = jnp.broadcast_to(remote[2:3], (8, ELEMS))
    index[7] = jnp.broadcast_to(remote[3:4], (8, ELEMS))

    for k in MIDDLE:
        loads[k].wait()
    y_copies.append(send_y(0, MIDDLE))

    loop(0, 8, lambda k: primitives(k, False))

    def along_k_first(i):
        at = lambda n: (n, rows_i(i))
        for c, flux in fluxes(2, at):
            rate = derivative(flux)
            for n in range(8):
                r[c, *at(n)] = rate[n]

    loop(0, 8, along_k_first)
    for k in ENDS:
        in_plane(k)
        surface_x(k)
    y_copies[0].wait_recv()
    surface_y(0, ENDS)

    for s, k in enumerate(ENDS):
        for i in range(8):
            for c in range(5):
                ends[s, c, i] = u[c, k, rows_i(i)] + STEP * r[c, k, rows_i(i)]
    z_copies += [
        send(2, ends.at[0], recv_z.at[2], below),
        send(3, ends.at[1], recv_z.at[3], above),
    ]

    loop(1, LAST, in_plane)
    loop(1, LAST, surface_x, 6)
    y_copies[1].wait_recv()
    surface_y(0, MIDDLE)

    loop(1, LAST, lambda k: primitives(k, True))
    y_copies.append(send_y(1, MIDDLE))
    loop(1, LAST, in_plane)

    def along_k_middle(i):
        at = lambda n: (n, rows_i(i))
        for c, flux in fluxes(2, at, MIDDLE):
            rate = derivative(flux, (1, 2, 3))
            for n in range(8):
                r[c, *at(n)] += rate[n]

    loop(0, 8, along_k_middle)
    loop(1, LAST, surface_x, 6)
    y_copies[2].wait_recv()
    surface_y(1, MIDDLE)

    for copy in z_copies[:2]:
        copy.wait()

    def surface_z_first(i):
        rows = rows_i(i)
        right = [pick(recv_z[0, c, i], index[5]) for c in range(5)]
        star = rusanov([u[c, LAST, rows] for c in range(5)], right, 2)
        for c in range(5):
            lifted = LIFT * star[c]
            star_z[0, c, i] = lifted
            r[c, LAST, rows] -= lifted
            u[c, LAST, rows] = ends[1, c, i] - STEP * lifted
        left = [pick(recv_z[1, c, i], index[4]) for c in range(5)]
        star = rusanov(left, [u[c, 0, rows] for c in range(5)], 2)
        for c in range(5):
            lifted = LIFT * star[c]
            star_z[1, c, i] = lifted
            r[c, 0, rows] += lifted
            u[c, 0, rows] = ends[0, c, i] + STEP * lifted

    loop(0, 8, surface_z_first, 8)
    y_copies.append(send_y(1, ENDS))
    for k in ENDS:
        primitives(k, False)
    for k in ENDS:
        in_plane(k)
        surface_x(k)

    def along_k_ends(i):
        at = lambda n: (n, rows_i(i))
        for c, flux in fluxes(2, at, ENDS):
            rate = derivative(flux, (0,))
            for n in ENDS:
                r[c, *at(n)] += rate[n]
            for n in MIDDLE:
                out[c, i, rows_k(n)] = (0.5 * STEP) * (r[c, *at(n)] + rate[n])

    loop(0, 8, along_k_ends)
    y_copies[3].wait_recv()
    surface_y(1, ENDS)

    for copy in z_copies[2:]:
        copy.wait_recv()

    def surface_z_second(i):
        rows = rows_i(i)
        right = [pick(recv_z[2, c, i], index[5]) + STEP * star_z[0, c, i] for c in range(5)]
        star = rusanov([u[c, LAST, rows] for c in range(5)], right, 2)
        for c in range(5):
            out[c, i, rows_k(LAST)] = (0.5 * STEP) * (r[c, LAST, rows] - LIFT * star[c])
        left = [pick(recv_z[3, c, i], index[4]) - STEP * star_z[1, c, i] for c in range(5)]
        star = rusanov(left, [u[c, 0, rows] for c in range(5)], 2)
        for c in range(5):
            out[c, i, rows_k(0)] = (0.5 * STEP) * (r[c, 0, rows] + LIFT * star[c])

    loop(0, 8, surface_z_second, 8)
    for copy in z_copies[2:]:
        copy.wait_send()
    for copy in y_copies:
        copy.wait_send()


def body(devices, state, neighbours):
    field = pltpu.VMEM((5, 8, 64, ELEMS), jnp.float32)
    faces = (5, 8, 8, ELEMS)
    change = pl.pallas_call(
        functools.partial(kernel, devices),
        out_shape=pltpu.VMEM((5, 8, 64, ELEMS), jnp.float32),
        in_specs=[pl.BlockSpec(memory_space=pltpu.HBM), pl.BlockSpec(memory_space=pltpu.HBM)],
        out_specs=pl.BlockSpec(memory_space=pltpu.VMEM),
        scratch_shapes=[
            pltpu.VMEM((5, 8, 8, 8, ELEMS), jnp.float32),
            field,
            field,
            pltpu.VMEM((6, ELEMS), jnp.int32),
            pltpu.VMEM((8, 8, ELEMS), jnp.int32),
            pltpu.VMEM((2,) + faces, jnp.float32),
            pltpu.VMEM((4,) + faces, jnp.float32),
            pltpu.VMEM((2,) + faces, jnp.float32),
            pltpu.VMEM((2, 2, 5, 2, 8, ELEMS), jnp.float32),
            pltpu.VMEM((2, 2, 5, 6, 8, ELEMS), jnp.float32),
            pltpu.VMEM((2, 2, 5, 2, 8, ELEMS), jnp.float32),
            pltpu.VMEM((2, 2, 5, 6, 8, ELEMS), jnp.float32),
            pltpu.SemaphoreType.DMA((9,)),
            pltpu.SemaphoreType.DMA((8,)),
            pltpu.SemaphoreType.DMA((8,)),
        ],
        compiler_params=pltpu.CompilerParams(
            collective_id=0, has_side_effects=True, vmem_limit_bytes=40 * 1024 * 1024
        ),
        cost_estimate=pl.CostEstimate(
            flops=25_000_000, bytes_accessed=2_700_000, transcendentals=0
        ),
    )(
        pltpu.with_memory_space_constraint(state, pltpu.HBM),
        pltpu.with_memory_space_constraint(neighbours, pltpu.HBM),
    )
    return change.reshape(state.shape)


def solution(mesh):
    devices = mesh.shape["dev"]
    in_specs = (P(None, None, None, None, "dev"), P(None, "dev"))
    out_specs = P(None, None, None, None, "dev")
    return jax.shard_map(
        functools.partial(body, devices),
        mesh=mesh,
        in_specs=in_specs,
        out_specs=out_specs,
        check_vma=False,
    )
```

```python
import functools

import jax
import jax.numpy as jnp
import numpy as np
from jax import lax
from jax.experimental import pallas as pl
from jax.experimental.pallas import tpu as pltpu
from jax.sharding import PartitionSpec as P

MESH = pl.DeviceIdType.MESH
GAMMA = 1.4
STEP = 0.003
NODES = 8
ELEMS = 128
LAST = NODES - 1
LIFT = LAST * (LAST + 1) / 2.0
ENDS = (0, LAST)
MIDDLE = tuple(range(1, LAST))
LOBATTO_EIGHT = (
    -1.0,
    -0.8717401485096066,
    -0.5917001814331423,
    -0.2092992179024789,
    0.2092992179024789,
    0.5917001814331423,
    0.8717401485096066,
    1.0,
)


def folded_matrix():
    points = np.array(LOBATTO_EIGHT)
    identity = np.eye(NODES)
    spacing = points[:, None] - points[None, :] + identity
    weights = 1.0 / np.prod(spacing, axis=1)
    matrix = weights[None, :] / weights[:, None] / spacing
    matrix = matrix * (1.0 - identity)
    matrix = matrix - identity * np.sum(matrix, axis=1)[:, None]
    matrix = -matrix
    matrix[LAST, LAST] += LIFT
    matrix[0, 0] -= LIFT
    return matrix


MATRIX = folded_matrix()
EVEN = 0.5 * (MATRIX[:4, :4] + MATRIX[:4, :3:-1])
ODD = 0.5 * (MATRIX[:4, :4] - MATRIX[:4, :3:-1])


def plane_matrix():
    identity = np.eye(NODES)
    two = np.concatenate([np.kron(MATRIX, identity), np.kron(identity, MATRIX)], axis=1)
    high = two.astype(np.float32).astype(jnp.bfloat16)
    low = (two - high.astype(np.float64)).astype(np.float32).astype(jnp.bfloat16)
    upper = np.concatenate([high, high], axis=1)
    lower = np.concatenate([low, np.zeros_like(low)], axis=1)
    return np.concatenate([upper, lower], axis=0)


def derivative(values, pairs=(0, 1, 2, 3)):
    even = {j: values[j] + values[LAST - j] for j in pairs}
    odd = {j: values[j] - values[LAST - j] for j in pairs}
    result = [None] * NODES
    for i in range(4):
        a = b = None
        for j in pairs:
            x = even[j] * float(EVEN[i, j])
            y = odd[j] * float(ODD[i, j])
            a = x if a is None else a + x
            b = y if b is None else b + y
        result[i] = b + a
        result[LAST - i] = b - a
    return result


def primitive(q):
    inverse = 1.0 / q[0]
    v = [q[1] * inverse, q[2] * inverse, q[3] * inverse]
    p = (GAMMA - 1.0) * (q[4] - 0.5 * (q[1] * v[0] + q[2] * v[1] + q[3] * v[2]))
    return inverse, v, p


def side(q, normal):
    inverse, v, p = primitive(q)
    speed = v[normal]
    flux = [q[1 + normal]]
    for column in range(3):
        term = q[1 + column] * speed
        flux.append(term + p if column == normal else term)
    flux.append((q[4] + p) * speed)
    wave = jnp.abs(speed) + jnp.sqrt(GAMMA * p * inverse)
    return flux, wave


def rusanov(left, right, normal):
    flux_left, wave_left = side(left, normal)
    flux_right, wave_right = side(right, normal)
    wave = jnp.maximum(wave_left, wave_right)
    return [
        0.5 * ((flux_left[c] + flux_right[c]) - wave * (right[c] - left[c])) for c in range(5)
    ]


def pick(table, columns):
    return jnp.take_along_axis(table, columns, axis=1, mode="promise_in_bounds")


def kernel(
    devices,
    state_hbm,
    neighbours_hbm,
    matrix_hbm,
    out,
    planes,
    r,
    prim,
    ids_ref,
    matrix,
    index,
    ends,
    recv_z,
    star_z,
    own_y_ends,
    own_y_middle,
    recv_y_ends,
    recv_y_middle,
    in_sem,
    send_sem,
    recv_sem,
):
    u = planes.reshape(5, 8, 64, ELEMS)
    me = lax.axis_index("dev")
    above = lax.rem(me + 2, devices)
    below = lax.rem(me + devices - 2, devices)
    partner = me + 1 - 2 * lax.rem(me, 2)

    loads = {
        k: pltpu.make_async_copy(state_hbm.at[:, :, :, k, :], planes.at[:, k], in_sem.at[k])
        for k in ENDS + MIDDLE
    }
    for k in ENDS:
        loads[k].start()
    load_ids = pltpu.make_async_copy(neighbours_hbm, ids_ref, in_sem.at[8])
    load_ids.start()
    load_matrix = pltpu.make_async_copy(matrix_hbm, matrix, in_sem.at[9])
    load_matrix.start()

    barrier = pltpu.get_barrier_semaphore()
    for other in (above, below, partner):
        pl.semaphore_signal(barrier, inc=1, device_id=(other,), device_id_type=MESH)

    def send(slot, source, target, device):
        copy = pltpu.make_async_remote_copy(
            src_ref=source,
            dst_ref=target,
            send_sem=send_sem.at[slot],
            recv_sem=recv_sem.at[slot],
            device_id=(device,),
            device_id_type=MESH,
        )
        copy.start()
        return copy

    def rows_i(i):
        if isinstance(i, int):
            return pl.ds(i * 8, 8)
        return pl.ds(pl.multiple_of(i * 8, 8), 8)

    def rows_j(j):
        return pl.ds(j, 8, stride=8)

    def rows_k(k):
        return pl.ds(k, 8, stride=8)

    def send_y(section, which):
        own, got, which_planes, slot = (
            (own_y_ends, recv_y_ends, ENDS, 4 + section)
            if which == ENDS
            else (own_y_middle, recv_y_middle, MIDDLE, 6 + section)
        )
        for n, k in enumerate(which_planes):
            for c in range(5):
                for side_y, j in ((0, 0), (1, LAST)):
                    own[section, side_y, c, n] = u[c, k, rows_j(j)]
        return send(slot, own.at[section], got.at[section], partner)

    def primitives(k, update):
        for i in range(8):
            q = [u[c, k, rows_i(i)] for c in range(5)]
            if update:
                q = [q[c] + STEP * r[c, k, rows_i(i)] for c in range(5)]
                for c in range(5):
                    u[c, k, rows_i(i)] = q[c]
            _, v, p = primitive(q)
            for d in range(3):
                prim[d, k, rows_i(i)] = v[d]
            prim[3, k, rows_i(i)] = p
            prim[4, k, rows_i(i)] = q[4] + p

    def fluxes(normal, at, nodes=tuple(range(8))):
        speed = {n: prim[normal, *at(n)] for n in nodes}
        for c in range(5):
            if c == 0:
                yield c, {n: u[1 + normal, *at(n)] for n in nodes}
                continue
            if c == 4:
                yield c, {n: prim[4, *at(n)] * speed[n] for n in nodes}
                continue
            flux = {n: u[c, *at(n)] * speed[n] for n in nodes}
            if c == 1 + normal:
                flux = {n: flux[n] + prim[3, *at(n)] for n in nodes}
            yield c, flux

    def in_plane(k):
        pairs = ((0, 1), (2, 3), (4,))
        whole = pl.ds(0, 64)
        for group in pairs:
            columns = []
            for c in group:
                tall = []
                for normal in range(2):
                    if c == 0:
                        flux = u[1 + normal, k, whole]
                    elif c == 4:
                        flux = prim[4, k, whole] * prim[normal, k, whole]
                    else:
                        flux = u[c, k, whole] * prim[normal, k, whole]
                        if c == 1 + normal:
                            flux = flux + prim[3, k, whole]
                    tall.append(flux)
                high = [flux.astype(jnp.bfloat16) for flux in tall]
                low = [
                    (flux - h.astype(jnp.float32)).astype(jnp.bfloat16)
                    for flux, h in zip(tall, high)
                ]
                columns.append(jnp.concatenate(high + low, axis=0))
            right = columns[0] if len(columns) == 1 else jnp.concatenate(columns, axis=1)
            both = jnp.dot(matrix[...], right, preferred_element_type=jnp.float32)
            for n, c in enumerate(group):
                lanes = slice(n * ELEMS, (n + 1) * ELEMS)
                r[c, k, whole] += both[:64, lanes] + both[64:, lanes]

    def surface_x(k):
        left = [u[c, k, rows_i(LAST)] for c in range(5)]
        right = [pick(u[c, k, rows_i(0)], index[1]) for c in range(5)]
        star = rusanov(left, right, 0)
        for c in range(5):
            lifted = LIFT * star[c]
            r[c, k, rows_i(LAST)] -= lifted
            r[c, k, rows_i(0)] += pick(lifted, index[0])

    def surface_y(section, which):
        own, got, which_planes = (
            (own_y_ends, recv_y_ends, ENDS)
            if which == ENDS
            else (own_y_middle, recv_y_middle, MIDDLE)
        )
        for n, k in enumerate(which_planes):
            lower = [own[section, 0, c, n] for c in range(5)]
            upper = [own[section, 1, c, n] for c in range(5)]
            remote_low = index[6] != 0
            remote_up = index[7] != 0
            right = [
                jnp.where(
                    remote_up, pick(got[section, 0, c, n], index[3]), pick(lower[c], index[3])
                )
                for c in range(5)
            ]
            star = rusanov(upper, right, 1)
            for c in range(5):
                r[c, k, rows_j(LAST)] = r[c, k, rows_j(LAST)] - LIFT * star[c]
            left = [
                jnp.where(
                    remote_low, pick(got[section, 1, c, n], index[2]), pick(upper[c], index[2])
                )
                for c in range(5)
            ]
            star = rusanov(left, lower, 1)
            for c in range(5):
                r[c, k, rows_j(0)] = r[c, k, rows_j(0)] + LIFT * star[c]

    def loop(first, last, step, unroll=1):
        def wrapped(n, carry):
            step(n)
            return carry

        lax.fori_loop(first, last, wrapped, 0, unroll=unroll)

    for k in ENDS:
        loads[k].wait()
    pl.semaphore_wait(barrier, 3)
    z_copies = [
        send(0, planes.at[:, 0], recv_z.at[0], below),
        send(1, planes.at[:, LAST], recv_z.at[1], above),
    ]
    for k in MIDDLE:
        loads[k].start()
    y_copies = [send_y(0, ENDS)]

    load_ids.wait()
    ids = ids_ref[...]
    local = jnp.bitwise_and(ids, ELEMS - 1)
    remote = (jnp.right_shift(ids, 7) != me).astype(jnp.int32)
    for f in range(6):
        index[f] = jnp.broadcast_to(local[f : f + 1], (8, ELEMS))
    index[6] = jnp.broadcast_to(remote[2:3], (8, ELEMS))
    index[7] = jnp.broadcast_to(remote[3:4], (8, ELEMS))

    for k in MIDDLE:
        loads[k].wait()
    y_copies.append(send_y(0, MIDDLE))

    loop(0, 8, lambda k: primitives(k, False))

    def along_k_first(i):
        at = lambda n: (n, rows_i(i))
        for c, flux in fluxes(2, at):
            rate = derivative(flux)
            for n in range(8):
                r[c, *at(n)] = rate[n]

    loop(0, 8, along_k_first)
    load_matrix.wait()
    for k in ENDS:
        in_plane(k)
        surface_x(k)
    y_copies[0].wait_recv()
    surface_y(0, ENDS)

    for s, k in enumerate(ENDS):
        for i in range(8):
            for c in range(5):
                ends[s, c, i] = u[c, k, rows_i(i)] + STEP * r[c, k, rows_i(i)]

    loop(1, LAST, in_plane, 6)
    loop(1, LAST, surface_x, 6)
    y_copies[1].wait_recv()
    surface_y(0, MIDDLE)
    for copy in z_copies[:2]:
        copy.wait_send()
    z_copies += [
        send(2, ends.at[0], recv_z.at[2], below),
        send(3, ends.at[1], recv_z.at[3], above),
    ]

    loop(1, LAST, lambda k: primitives(k, True))
    y_copies.append(send_y(1, MIDDLE))
    loop(1, LAST, in_plane, 6)

    def along_k_middle(i):
        at = lambda n: (n, rows_i(i))
        for c, flux in fluxes(2, at, MIDDLE):
            rate = derivative(flux, (1, 2, 3))
            for n in range(8):
                r[c, *at(n)] += rate[n]

    loop(0, 8, along_k_middle)
    loop(1, LAST, surface_x, 6)
    y_copies[2].wait_recv()
    surface_y(1, MIDDLE)

    for copy in z_copies[:2]:
        copy.wait_recv()

    def surface_z_first(i):
        rows = rows_i(i)
        right = [pick(recv_z[0, c, i], index[5]) for c in range(5)]
        star = rusanov([u[c, LAST, rows] for c in range(5)], right, 2)
        for c in range(5):
            lifted = LIFT * star[c]
            star_z[0, c, i] = lifted
            r[c, LAST, rows] -= lifted
            u[c, LAST, rows] = ends[1, c, i] - STEP * lifted
        left = [pick(recv_z[1, c, i], index[4]) for c in range(5)]
        star = rusanov(left, [u[c, 0, rows] for c in range(5)], 2)
        for c in range(5):
            lifted = LIFT * star[c]
            star_z[1, c, i] = lifted
            r[c, 0, rows] += lifted
            u[c, 0, rows] = ends[0, c, i] + STEP * lifted

    loop(0, 8, surface_z_first, 8)
    y_copies.append(send_y(1, ENDS))
    for k in ENDS:
        primitives(k, False)
    for k in ENDS:
        in_plane(k)
        surface_x(k)

    def along_k_ends(i):
        at = lambda n: (n, rows_i(i))
        for c, flux in fluxes(2, at, ENDS):
            rate = derivative(flux, (0,))
            for n in ENDS:
                r[c, *at(n)] += rate[n]
            for n in MIDDLE:
                out[c, i, rows_k(n)] = (0.5 * STEP) * (r[c, *at(n)] + rate[n])

    loop(0, 8, along_k_ends)
    y_copies[3].wait_recv()
    surface_y(1, ENDS)

    for copy in z_copies[2:]:
        copy.wait_recv()

    def surface_z_second(i):
        rows = rows_i(i)
        right = [pick(recv_z[2, c, i], index[5]) + STEP * star_z[0, c, i] for c in range(5)]
        star = rusanov([u[c, LAST, rows] for c in range(5)], right, 2)
        for c in range(5):
            out[c, i, rows_k(LAST)] = (0.5 * STEP) * (r[c, LAST, rows] - LIFT * star[c])
        left = [pick(recv_z[3, c, i], index[4]) - STEP * star_z[1, c, i] for c in range(5)]
        star = rusanov(left, [u[c, 0, rows] for c in range(5)], 2)
        for c in range(5):
            out[c, i, rows_k(0)] = (0.5 * STEP) * (r[c, 0, rows] + LIFT * star[c])

    loop(0, 8, surface_z_second, 8)
    for copy in z_copies[2:]:
        copy.wait_send()
    for copy in y_copies:
        copy.wait_send()


def body(devices, state, neighbours):
    field = pltpu.VMEM((5, 8, 64, ELEMS), jnp.float32)
    faces = (5, 8, 8, ELEMS)
    change = pl.pallas_call(
        functools.partial(kernel, devices),
        out_shape=pltpu.VMEM((5, 8, 64, ELEMS), jnp.float32),
        in_specs=[pl.BlockSpec(memory_space=pltpu.HBM)] * 3,
        out_specs=pl.BlockSpec(memory_space=pltpu.VMEM),
        scratch_shapes=[
            pltpu.VMEM((5, 8, 8, 8, ELEMS), jnp.float32),
            field,
            field,
            pltpu.VMEM((6, ELEMS), jnp.int32),
            pltpu.VMEM((128, 256), jnp.bfloat16),
            pltpu.VMEM((8, 8, ELEMS), jnp.int32),
            pltpu.VMEM((2,) + faces, jnp.float32),
            pltpu.VMEM((4,) + faces, jnp.float32),
            pltpu.VMEM((2,) + faces, jnp.float32),
            pltpu.VMEM((2, 2, 5, 2, 8, ELEMS), jnp.float32),
            pltpu.VMEM((2, 2, 5, 6, 8, ELEMS), jnp.float32),
            pltpu.VMEM((2, 2, 5, 2, 8, ELEMS), jnp.float32),
            pltpu.VMEM((2, 2, 5, 6, 8, ELEMS), jnp.float32),
            pltpu.SemaphoreType.DMA((10,)),
            pltpu.SemaphoreType.DMA((8,)),
            pltpu.SemaphoreType.DMA((8,)),
        ],
        compiler_params=pltpu.CompilerParams(
            collective_id=0, has_side_effects=True, vmem_limit_bytes=40 * 1024 * 1024
        ),
        cost_estimate=pl.CostEstimate(
            flops=25_000_000, bytes_accessed=2_700_000, transcendentals=0
        ),
    )(
        pltpu.with_memory_space_constraint(state, pltpu.HBM),
        pltpu.with_memory_space_constraint(neighbours, pltpu.HBM),
        pltpu.with_memory_space_constraint(jnp.asarray(plane_matrix()), pltpu.HBM),
    )
    return change.reshape(state.shape)


def solution(mesh):
    devices = mesh.shape["dev"]
    in_specs = (P(None, None, None, None, "dev"), P(None, "dev"))
    out_specs = P(None, None, None, None, "dev")
    return jax.shard_map(
        functools.partial(body, devices),
        mesh=mesh,
        in_specs=in_specs,
        out_specs=out_specs,
        check_vma=False,
    )
```
